1024 devices in a mesh: row: 64 (over y, x_hi, core), col: 16 (over z, x_lo).
Axes of the slice: x: 8 (x_hi: 4, x_lo: 2; x = x_hi * 2 + x_lo), y: 8, z: 8, core: 2. Of those that a mesh axis runs over, the one named last changes fastest.
Arguments:
- a_blocks: bfloat16 [16, 64, 128, 128], P('col', 'row'), may hold values from -6 to 6
- a_rows: int32 [16, 64], P('col', 'row'), may hold values from 0 to 1, as said below
- b_blocks: bfloat16 [2, 64, 64, 128, 128], P(None, 'row', 'col'), may hold values from -0.25 to 0.25
- b_cols: int32 [2, 64, 64], P(None, 'row', 'col'), may hold values from 0 to 15
- owner: int32 [16, 64, 16], P('col', 'row'), may hold values from 0 to 15, each once within a row
Outputs:
- delivered: bfloat16 [2, 16, 64, 16, 128, 128], P(None, 'col', 'row')
The draws below stay inside these ranges and needn't reach their ends.
Inputs may be any that keep to these rules, and one draw needn't show every extreme that they name: `a_rows`: A value below 1 is the block row of the panel's one occupied block; 1 marks a panel without a block. `owner`: each panel pair's last dimension is a permutation of 0 to 15.
All inputs are finite; a program needn't handle non-finite values.
Results may differ from the reference program's by a relative error of at most 0.001.
Values may be sent and summed in bfloat16 or wider, within the bound.
No kernel may reach another device: no remote copies, remote signals or barrier semaphores. Data moves between devices by JAX's collectives and lax.ppermute only.
A program may use at most 64 MiB of HBM per device.

```python
import jax
import jax.numpy as jnp
from jax import lax

BLK = 128
LB = 16
BR = 1
NCB = 16
N_ROW = 64
N_COL = 16


def draw_a_rows(key, part):
    key = jax.random.fold_in(key, 11)
    first_key, second_key = jax.random.split(key)
    shape = (N_COL, N_ROW)
    panel = lax.broadcasted_iota(jnp.int32, shape, 0)
    gauge = jax.random.randint(first_key, shape, 0, N_COL, dtype=jnp.int32)
    block = jax.random.randint(second_key, shape, 0, BR, dtype=jnp.int32)
    return jnp.where(gauge < panel, BR, block).astype(jnp.int32)


def set_ends(result, own_key, smallest, largest):
    dims = result.shape
    place = [jax.random.randint(jax.random.fold_in(own_key, axis), (), 0, dims[axis]) for axis in range(len(dims))]
    result = result.at[tuple(place)].set(smallest)
    longest = dims.index(max(dims))
    place[longest] = (place[longest] + 1) % dims[longest]
    return result.at[tuple(place)].set(largest)


def shard_levels(key, dims, cuts, smallest, largest):
    loudness, own = 1.0, jax.random.fold_in(key, 6)
    for dim, shards_of in cuts:
        steps = jnp.exp(jax.random.uniform(jax.random.fold_in(own, dim), (shards_of,), jnp.float32, smallest / len(cuts), largest / len(cuts)))
        loudness = loudness * jnp.repeat(steps, dims[dim] // shards_of).reshape([-1 if axis == dim else 1 for axis in range(len(dims))])
    return loudness


def centred(stream_key, shape, spread, reach, cuts=(), kind=jnp.bfloat16):
    result = jax.random.normal(stream_key, shape, jnp.float32) * spread
    if len(cuts) > 0:
        result = shard_levels(stream_key, shape, cuts, -0.22, 0.18) * result
    return jnp.clip(result, min=-reach, max=reach).astype(kind)


def setup_inputs(seed: int = 0) -> dict:
    arg_keys = jax.random.split(jax.random.key(seed), 6)
    a_blocks = centred(arg_keys[0], (N_COL, N_ROW, BLK, BLK), 1.0, 6.0, ((0, 16), (1, 64)))
    a_rows = draw_a_rows(jax.random.fold_in(arg_keys[5], 71), 0)
    b_blocks = centred(arg_keys[2], (2, N_ROW, N_ROW, BLK, BLK), (BLK * 4) ** -0.5, 0.25, ((1, 64), (2, 16)))
    b_cols = set_ends(jax.random.randint(arg_keys[3], (2, N_ROW, N_ROW), 0, LB), jax.random.fold_in(arg_keys[3], 1), 0, LB - 1).astype(jnp.int32)
    owner = jax.vmap(lambda own: jax.random.permutation(own, NCB))(jax.random.split(arg_keys[4], N_COL * N_ROW)).reshape((N_COL, N_ROW, NCB)).astype(jnp.int32)
    return dict(a_blocks=a_blocks, a_rows=a_rows, b_blocks=b_blocks, b_cols=b_cols, owner=owner)


def reference(a_blocks, a_rows, b_blocks, b_cols, owner):
    panels = N_ROW
    group_size = N_ROW // N_COL
    per_dest = NCB // N_COL
    k_panel = jnp.arange(panels, dtype=jnp.int32)
    slots = jnp.arange(NCB, dtype=jnp.int32)

    def one_panel(flat):
        my_col = (flat // panels).astype(jnp.int32)
        my_row = (flat % panels).astype(jnp.int32)
        source_row = ((group_size * my_col - k_panel) % panels).astype(jnp.int32)
        slab = a_blocks[my_col][source_row].astype(jnp.float32)
        block_rows = a_rows[my_col][source_row]
        stored_at = ((k_panel + my_row) % panels).astype(jnp.int32)
        square = b_blocks[:, my_row][:, stored_at].astype(jnp.float32)
        block_cols = b_cols[:, my_row][:, stored_at]
        products = jnp.einsum("kij,okjl->okil", slab, square)
        occupied = block_rows < BR
        target_slot = block_rows[None, :] * LB + block_cols
        selector = jnp.logical_and(target_slot[:, :, None] == slots[None, None, :], occupied[None, :, None]).astype(jnp.float32)
        totals = jnp.einsum("oks,okil->osil", selector, products, precision=lax.Precision.HIGHEST)
        send_order = jnp.argsort(owner[my_col, my_row]).astype(jnp.int32)
        return totals.astype(jnp.bfloat16)[:, send_order]

    stacked = lax.map(one_panel, jnp.arange(N_COL * N_ROW, dtype=jnp.int32))
    stacked = stacked.reshape(N_COL, N_ROW, 2, N_COL, per_dest, BLK, BLK)
    stacked = jnp.transpose(stacked, (2, 3, 1, 0, 4, 5, 6))
    return stacked.reshape(2, N_COL, N_ROW, NCB, BLK, BLK)
```

```python
import jax
import jax.numpy as jnp
from jax import lax
from jax.experimental import pallas as pl
from jax.experimental.pallas import tpu as pltpu
from jax.sharding import Mesh
from jax.sharding import PartitionSpec as P

BR = 1
CORES = 2
X_LO = 2
X_HI = 4
ROW = ("y", "x_hi", "core")
COL = ("z", "x_lo")


def multiply(place_ref, owner_ref, own_ref, partner_ref, *refs):
    b_refs, (out_ref, total, label_rows, labels, arrived) = refs[:-5], refs[-5:]
    cores, half = CORES, own_ref.shape[0]
    panels = cores * half
    edge = own_ref.shape[1]
    sides = [side for ref in b_refs for side in ([ref] if len(ref.shape) == 2 else [ref.at[i] for i in range(ref.shape[0])])]
    planes = len(sides) // X_LO
    group = panels // len(sides)
    for n, side_ref in enumerate(sides):
        row = side_ref[pl.ds(2 * group * edge, 16), :].astype(jnp.float32)[:8]
        label_rows[pl.ds(8 * n, 8), :] = row.astype(jnp.int32)
    copy = pltpu.make_async_copy(label_rows, labels, arrived)
    copy.start()
    total[...] = jnp.zeros_like(total)
    copy.wait()
    base, here, core = place_ref[0], place_ref[1], place_ref[2]

    for n, side_ref in enumerate(sides):
        plane = lax.rem(here + planes - n // X_LO, planes)
        for j in range(group):
            m = (plane * X_LO + n % X_LO) * group + j
            q = lax.rem(base + panels - m, panels)
            mine = lax.rem(q, cores) == core
            a = jnp.where(mine, own_ref[q // cores], partner_ref[q // cores])
            for o in range(2):
                target = owner_ref[labels[8 * n, o * group + j]]
                b = side_ref[pl.ds((o * group + j) * edge, edge), :]
                total[target, o] += jnp.dot(a, b, preferred_element_type=jnp.float32)
    out_ref[...] = total[...].astype(out_ref.dtype)


def block_products(place, owner, a_own, a_partner, b_pieces):
    slots, edge = owner.shape[0], a_own.shape[-1]
    smem = pl.BlockSpec(memory_space=pltpu.SMEM)
    vmem = pl.BlockSpec(memory_space=pltpu.VMEM)
    label_shape = (8 * lax.axis_size(COL), edge)
    return pl.pallas_call(
        multiply,
        out_shape=jax.ShapeDtypeStruct((slots, 2, edge, edge), jnp.bfloat16),
        in_specs=[smem, smem] + [vmem] * (2 + len(b_pieces)),
        out_specs=vmem,
        scratch_shapes=[
            pltpu.VMEM((slots, 2, edge, edge), jnp.float32),
            pltpu.VMEM(label_shape, jnp.int32),
            pltpu.SMEM(label_shape, jnp.int32),
            pltpu.SemaphoreType.DMA,
        ],
        compiler_params=pltpu.CompilerParams(vmem_limit_bytes=24 * 1024 * 1024),
    )(place, owner, a_own, a_partner, *b_pieces)


def around(piece, axis):
    n = lax.axis_size(axis)
    up = [(i, (i + 1) % n) for i in range(n)]
    down = [(i, (i - 1) % n) for i in range(n)]
    found = [piece] + [None] * (n - 1)
    for t in range(1, (n - 1) // 2 + 1):
        found[t] = lax.ppermute(found[t - 1], axis, up)
        found[n - t] = lax.ppermute(found[(n - t + 1) % n], axis, down)
    far = n // 2
    found[far : far + 1] = [
        lax.ppermute(found[far - 1][0], axis, up),
        lax.ppermute(found[(far + 1) % n][1], axis, down),
    ]
    return found


def shards(a_blocks, a_rows, b_blocks, b_cols, owner):
    edge = a_blocks.shape[-1]
    panels = lax.axis_size(ROW)
    group = b_blocks.shape[2]
    a_own = jnp.where(a_rows[0, 0] < BR, a_blocks[0, 0], jnp.zeros_like(a_blocks[0, 0]))
    labels = jnp.pad(b_cols.reshape(1, -1).astype(jnp.bfloat16), ((0, 15), (0, edge - 2 * group)))
    b_own = jnp.concatenate([b_blocks.reshape(-1, edge), labels])

    a_line = lax.all_gather(a_own, "x_hi", axis=0)
    n_y = lax.axis_size("y")
    a_half = lax.all_to_all(
        jnp.broadcast_to(a_line[None], (n_y,) + a_line.shape), "y", split_axis=0, concat_axis=0, tiled=True
    ).reshape(-1, edge, edge)
    partner = lax.ppermute(a_half, "core", [(0, 1), (1, 0)])

    b_pieces = around(lax.all_gather(b_own, "x_lo", axis=0), "z")
    base = (group * lax.axis_index(COL) + lax.axis_index(ROW)) % panels
    place = jnp.stack([base, lax.axis_index("z"), lax.axis_index("core")]).astype(jnp.int32)
    outgoing = block_products(place, owner[0, 0], a_half, partner, b_pieces)
    arrived = lax.all_to_all(outgoing, COL, split_axis=0, concat_axis=0, tiled=True)
    return jnp.swapaxes(arrived, 0, 1)[:, None, None]


def solution(mesh):
    rows, columns = mesh.devices.shape
    fine = Mesh(
        mesh.devices.reshape(rows // (X_HI * CORES), X_HI, CORES, columns // X_LO, X_LO), ROW + COL
    )
    in_specs = (
        P(COL, ROW, None, None),
        P(COL, ROW),
        P(None, ROW, COL, None, None),
        P(None, ROW, COL),
        P(COL, ROW, None),
    )
    out_specs = P(None, COL, ROW, None, None, None)
    return jax.shard_map(shards, mesh=fine, in_specs=in_specs, out_specs=out_specs, check_vma=False)
```

```python
import functools

import jax
import jax.numpy as jnp
from jax import lax
from jax.experimental import pallas as pl
from jax.experimental.pallas import tpu as pltpu
from jax.sharding import Mesh
from jax.sharding import PartitionSpec as P

BR = 1
CORES = 2
X_LO = 2
X_HI = 4
ROW = ("y", "x_hi", "core")
COL = ("z", "x_lo")


def add_products(place_ref, owner_ref, own_ref, partner_ref, sides, total, label_rows, labels, arrived):
    cores, half = CORES, own_ref.shape[0]
    panels = cores * half
    edge = own_ref.shape[1]
    group = (sides[0][2].shape[0] // edge) // 2
    for n, (_, _, side_ref) in enumerate(sides):
        row = side_ref[pl.ds(2 * group * edge, 16), :].astype(jnp.float32)[:8]
        label_rows[pl.ds(8 * n, 8), :] = row.astype(jnp.int32)
    copy = pltpu.make_async_copy(label_rows, labels, arrived)
    copy.start()
    total[...] = jnp.zeros_like(total)
    copy.wait()
    base, here, core = place_ref[0], place_ref[1], place_ref[2]
    planes = panels // (group * X_LO)

    for n, (away, low, side_ref) in enumerate(sides):
        plane = lax.rem(here + planes - away, planes)
        for j in range(group):
            m = (plane * X_LO + low) * group + j
            q = lax.rem(base + panels - m, panels)
            mine = lax.rem(q, cores) == core
            a = jnp.where(mine, own_ref[q // cores], partner_ref[q // cores])
            for o in range(2):
                target = owner_ref[labels[8 * n, o * group + j]]
                b = side_ref[pl.ds((o * group + j) * edge, edge), :]
                total[target, o] += jnp.dot(a, b, preferred_element_type=jnp.float32)


def near_products(aways, place_ref, owner_ref, own_ref, partner_ref, *refs):
    b_refs, (out_ref, *scratch) = refs[: len(aways)], refs[len(aways) :]
    sides = [(away, low, ref.at[low]) for away, ref in zip(aways, b_refs) for low in range(X_LO)]
    add_products(place_ref, owner_ref, own_ref, partner_ref, sides, out_ref, *scratch)


def far_products(away, place_ref, owner_ref, own_ref, partner_ref, near_ref, *refs):
    b_refs, (out_ref, total, *scratch) = refs[:X_LO], refs[X_LO:]
    sides = [(away, low, ref) for low, ref in enumerate(b_refs)]
    add_products(place_ref, owner_ref, own_ref, partner_ref, sides, total, *scratch)
    out_ref[...] = (near_ref[...] + total[...]).astype(out_ref.dtype)


def block_products(place, owner, a_own, a_partner, b_pieces):
    slots, edge = owner.shape[0], a_own.shape[-1]
    smem = pl.BlockSpec(memory_space=pltpu.SMEM)
    vmem = pl.BlockSpec(memory_space=pltpu.VMEM)
    far = len(b_pieces) // 2
    aways = [t for t in range(len(b_pieces)) if t != far]
    shape = (slots, 2, edge, edge)

    def scratch(sides):
        return [
            pltpu.VMEM((8 * sides, edge), jnp.int32),
            pltpu.SMEM((8 * sides, edge), jnp.int32),
            pltpu.SemaphoreType.DMA,
        ]

    def cost(sides):
        products = 2 * sides * (b_pieces[0].shape[1] // edge // 2)
        return pl.CostEstimate(flops=8 * products * edge**3, bytes_accessed=2**20, transcendentals=0)

    common = (place, owner, a_own, a_partner)
    near = pl.pallas_call(
        functools.partial(near_products, aways),
        out_shape=jax.ShapeDtypeStruct(shape, jnp.float32),
        in_specs=[smem, smem, vmem, vmem] + [vmem] * len(aways),
        out_specs=vmem,
        scratch_shapes=scratch(X_LO * len(aways)),
        compiler_params=pltpu.CompilerParams(vmem_limit_bytes=6 * 1024 * 1024),
        cost_estimate=cost(X_LO * len(aways)),
    )(*common, *[b_pieces[t] for t in aways])
    return pl.pallas_call(
        functools.partial(far_products, far),
        out_shape=jax.ShapeDtypeStruct(shape, jnp.bfloat16),
        in_specs=[smem, smem, vmem, vmem, vmem] + [vmem] * X_LO,
        out_specs=vmem,
        scratch_shapes=[pltpu.VMEM(shape, jnp.float32)] + scratch(X_LO),
        compiler_params=pltpu.CompilerParams(vmem_limit_bytes=6 * 1024 * 1024),
        cost_estimate=cost(X_LO),
    )(*common, near, *b_pieces[far])


def around(piece, axis):
    n = lax.axis_size(axis)
    up = [(i, (i + 1) % n) for i in range(n)]
    down = [(i, (i - 1) % n) for i in range(n)]
    found = [piece] + [None] * (n - 1)
    for t in range(1, (n - 1) // 2 + 1):
        found[t] = lax.ppermute(found[t - 1], axis, up)
        found[n - t] = lax.ppermute(found[(n - t + 1) % n], axis, down)
    far = n // 2
    found[far] = (
        lax.ppermute(found[far - 1][0], axis, up),
        lax.ppermute(found[(far + 1) % n][1], axis, down),
    )
    return found


def shards(a_blocks, a_rows, b_blocks, b_cols, owner):
    edge = a_blocks.shape[-1]
    panels = lax.axis_size(ROW)
    group = b_blocks.shape[2]
    a_own = jnp.where(a_rows[0, 0] < BR, a_blocks[0, 0], jnp.zeros_like(a_blocks[0, 0]))
    labels = jnp.pad(b_cols.reshape(1, -1).astype(jnp.bfloat16), ((0, 15), (0, edge - 2 * group)))
    b_own = jnp.concatenate([b_blocks.reshape(-1, edge), labels])

    b_other = lax.ppermute(b_own, "x_lo", [(0, 1), (1, 0)])
    low = lax.axis_index("x_lo")
    b_pair = jnp.where(low == 0, jnp.stack([b_own, b_other]), jnp.stack([b_other, b_own]))
    plane = ("y", "x_hi")
    a_half = lax.all_to_all(
        jnp.broadcast_to(a_own[None], (lax.axis_size(plane),) + a_own.shape), plane, split_axis=0, concat_axis=0, tiled=True
    )
    partner = lax.ppermute(a_half, "core", [(0, 1), (1, 0)])

    b_pieces = around(b_pair, "z")
    base = (group * lax.axis_index(COL) + lax.axis_index(ROW)) % panels
    place = jnp.stack([base, lax.axis_index("z"), lax.axis_index("core")]).astype(jnp.int32)
    outgoing = block_products(place, owner[0, 0], a_half, partner, b_pieces)
    arrived = lax.all_to_all(outgoing, COL, split_axis=0, concat_axis=0, tiled=True)
    return jnp.swapaxes(arrived, 0, 1)[:, None, None]


def solution(mesh):
    rows, columns = mesh.devices.shape
    fine = Mesh(
        mesh.devices.reshape(rows // (X_HI * CORES), X_HI, CORES, columns // X_LO, X_LO), ROW + COL
    )
    in_specs = (
        P(COL, ROW, None, None),
        P(COL, ROW),
        P(None, ROW, COL, None, None),
        P(None, ROW, COL),
        P(COL, ROW, None),
    )
    out_specs = P(None, COL, ROW, None, None, None)
    return jax.shard_map(shards, mesh=fine, in_specs=in_specs, out_specs=out_specs, check_vma=False)
```

```python
import functools

import jax
import jax.numpy as jnp
from jax import lax
from jax.experimental import pallas as pl
from jax.experimental.pallas import tpu as pltpu
from jax.sharding import Mesh
from jax.sharding import PartitionSpec as P

BR = 1
CORES = 2
X_LO = 2
X_HI = 4
ROW = ("y", "x_hi", "core")
COL = ("z", "x_lo")


def add_products(place_ref, owner_ref, own_ref, partner_ref, sides, start_ref, total, label_rows, labels, arrived):
    cores, half = CORES, own_ref.shape[0]
    panels = cores * half
    edge = own_ref.shape[1]
    group = (sides[0][2].shape[0] // edge) // 2
    for n, (_, _, side_ref) in enumerate(sides):
        row = side_ref[pl.ds(2 * group * edge, 16), :].astype(jnp.float32)[:8]
        label_rows[pl.ds(8 * n, 8), :] = row.astype(jnp.int32)
    copy = pltpu.make_async_copy(label_rows, labels, arrived)
    copy.start()
    total[...] = jnp.zeros_like(total) if start_ref is None else start_ref[...]
    copy.wait()
    base, here, core = place_ref[0], place_ref[1], place_ref[2]
    planes = panels // (group * X_LO)

    for n, (away, low, side_ref) in enumerate(sides):
        plane = lax.rem(here + planes - away, planes)
        for j in range(group):
            m = (plane * X_LO + low) * group + j
            q = lax.rem(base + panels - m, panels)
            mine = lax.rem(q, cores) == core
            chip = q // cores
            at = lax.rem(chip, X_HI) * (half // X_HI) + chip // X_HI
            a = jnp.where(mine, own_ref[at], partner_ref[at])
            for o in range(2):
                target = owner_ref[labels[8 * n, o * group + j]]
                b = side_ref[pl.ds((o * group + j) * edge, edge), :]
                total[target, o] += jnp.dot(a, b, preferred_element_type=jnp.float32)


def near_products(aways, place_ref, owner_ref, own_ref, partner_ref, *refs):
    b_refs, (out_ref, *scratch) = refs[: len(aways)], refs[len(aways) :]
    sides = [(away, low, ref.at[low]) for away, ref in zip(aways, b_refs) for low in range(X_LO)]
    add_products(place_ref, owner_ref, own_ref, partner_ref, sides, None, out_ref, *scratch)


def far_products(away, place_ref, owner_ref, own_ref, partner_ref, near_ref, *refs):
    b_refs, (out_ref, total, *scratch) = refs[:X_LO], refs[X_LO:]
    sides = [(away, low, ref) for low, ref in enumerate(b_refs)]
    add_products(place_ref, owner_ref, own_ref, partner_ref, sides, near_ref, total, *scratch)
    out_ref[...] = total[...].astype(out_ref.dtype)


def block_products(place, owner, a_own, a_partner, b_pieces):
    slots, edge = owner.shape[0], a_own.shape[-1]
    smem = pl.BlockSpec(memory_space=pltpu.SMEM)
    vmem = pl.BlockSpec(memory_space=pltpu.VMEM)
    far = len(b_pieces) // 2
    aways = [t for t in range(len(b_pieces)) if t != far]
    shape = (slots, 2, edge, edge)

    def scratch(sides):
        return [
            pltpu.VMEM((8 * sides, edge), jnp.int32),
            pltpu.SMEM((8 * sides, edge), jnp.int32),
            pltpu.SemaphoreType.DMA,
        ]

    def cost(sides):
        products = 2 * sides * (b_pieces[0].shape[1] // edge // 2)
        return pl.CostEstimate(flops=8 * products * edge**3, bytes_accessed=2**20, transcendentals=0)

    common = (place, owner, a_own, a_partner)
    near = pl.pallas_call(
        functools.partial(near_products, aways),
        out_shape=jax.ShapeDtypeStruct(shape, jnp.float32),
        in_specs=[smem, smem, vmem, vmem] + [vmem] * len(aways),
        out_specs=vmem,
        scratch_shapes=scratch(X_LO * len(aways)),
        compiler_params=pltpu.CompilerParams(vmem_limit_bytes=6 * 1024 * 1024),
        cost_estimate=cost(X_LO * len(aways)),
    )(*common, *[b_pieces[t] for t in aways])
    return pl.pallas_call(
        functools.partial(far_products, far),
        out_shape=jax.ShapeDtypeStruct(shape, jnp.bfloat16),
        in_specs=[smem, smem, vmem, vmem, vmem] + [vmem] * X_LO,
        out_specs=vmem,
        scratch_shapes=[pltpu.VMEM(shape, jnp.float32)] + scratch(X_LO),
        compiler_params=pltpu.CompilerParams(vmem_limit_bytes=6 * 1024 * 1024),
        cost_estimate=cost(X_LO),
    )(*common, near, *b_pieces[far])


def around(piece, axis):
    n = lax.axis_size(axis)
    up = [(i, (i + 1) % n) for i in range(n)]
    down = [(i, (i - 1) % n) for i in range(n)]
    found = [piece] + [None] * (n - 1)
    for t in range(1, (n - 1) // 2 + 1):
        found[t] = lax.ppermute(found[t - 1], axis, up)
        found[n - t] = lax.ppermute(found[(n - t + 1) % n], axis, down)
    far = n // 2
    found[far] = (
        lax.ppermute(found[far - 1][0], axis, up),
        lax.ppermute(found[(far + 1) % n][1], axis, down),
    )
    return found


def shards(a_blocks, a_rows, b_blocks, b_cols, owner):
    edge = a_blocks.shape[-1]
    panels = lax.axis_size(ROW)
    group = b_blocks.shape[2]
    a_own = jnp.where(a_rows[0, 0] < BR, a_blocks[0, 0], jnp.zeros_like(a_blocks[0, 0]))
    labels = jnp.pad(b_cols.reshape(1, -1).astype(jnp.bfloat16), ((0, 15), (0, edge - 2 * group)))
    b_own = jnp.concatenate([b_blocks.reshape(-1, edge), labels])

    b_other = lax.ppermute(b_own, "x_lo", [(0, 1), (1, 0)])
    low = lax.axis_index("x_lo")
    b_pair = jnp.where(low == 0, jnp.stack([b_own, b_other]), jnp.stack([b_other, b_own]))
    plane = ("x_hi", "y")
    a_half = lax.all_to_all(
        jnp.broadcast_to(a_own[None], (lax.axis_size(plane),) + a_own.shape), plane, split_axis=0, concat_axis=0, tiled=True
    )
    partner = lax.ppermute(a_half, "core", [(0, 1), (1, 0)])

    b_pieces = around(b_pair, "z")
    base = (group * lax.axis_index(COL) + lax.axis_index(ROW)) % panels
    place = jnp.stack([base, lax.axis_index("z"), lax.axis_index("core")]).astype(jnp.int32)
    outgoing = block_products(place, owner[0, 0], a_half, partner, b_pieces)
    arrived = lax.all_to_all(outgoing, COL, split_axis=0, concat_axis=0, tiled=True)
    return jnp.swapaxes(arrived, 0, 1)[:, None, None]


def solution(mesh):
    rows, columns = mesh.devices.shape
    fine = Mesh(
        mesh.devices.reshape(rows // (X_HI * CORES), X_HI, CORES, columns // X_LO, X_LO), ROW + COL
    )
    in_specs = (
        P(COL, ROW, None, None),
        P(COL, ROW),
        P(None, ROW, COL, None, None),
        P(None, ROW, COL),
        P(COL, ROW, None),
    )
    out_specs = P(None, COL, ROW, None, None, None)
    return jax.shard_map(shards, mesh=fine, in_specs=in_specs, out_specs=out_specs, check_vma=False)
```

```python
import functools

import jax
import jax.numpy as jnp
from jax import lax
from jax.experimental import pallas as pl
from jax.experimental.pallas import tpu as pltpu
from jax.sharding import Mesh
from jax.sharding import PartitionSpec as P

BR = 1
CORES = 2
X_LO = 2
X_HI = 4
ROW = ("y", "x_hi", "core")
COL = ("z", "x_lo")


def add_products(place_ref, owner_ref, own_ref, partner_ref, sides, start_ref, total, label_rows, labels, arrived):
    cores, half = CORES, own_ref.shape[0]
    panels = cores * half
    edge = own_ref.shape[1]
    group = (sides[0][2].shape[0] // edge) // 2
    for n, (_, _, side_ref) in enumerate(sides):
        row = side_ref[pl.ds(2 * group * edge, 16), :].astype(jnp.float32)[:8]
        label_rows[pl.ds(8 * n, 8), :] = row.astype(jnp.int32)
    copy = pltpu.make_async_copy(label_rows, labels, arrived)
    copy.start()
    total[...] = jnp.zeros_like(total) if start_ref is None else start_ref[...]
    copy.wait()
    base, here, core = place_ref[0], place_ref[1], place_ref[2]
    planes = panels // (group * X_LO)

    for n, (away, low, side_ref) in enumerate(sides):
        plane = lax.rem(here + planes - away, planes)
        for j in range(group):
            m = (plane * X_LO + low) * group + j
            q = lax.rem(base + panels - m, panels)
            mine = lax.rem(q, cores) == core
            chip = q // cores
            at = lax.rem(chip, X_HI) * (half // X_HI) + chip // X_HI
            a = jnp.where(mine, own_ref[at], partner_ref[at])
            for o in range(2):
                place = owner_ref[labels[8 * n, o * group + j]]
                target = lax.rem(place, X_LO) * (total.shape[0] // X_LO) + place // X_LO
                b = side_ref[pl.ds((o * group + j) * edge, edge), :]
                total[target, o] += jnp.dot(a, b, preferred_element_type=jnp.float32)


def near_products(aways, place_ref, owner_ref, own_ref, partner_ref, *refs):
    b_refs, (out_ref, *scratch) = refs[: len(aways)], refs[len(aways) :]
    sides = [(away, low, ref.at[low]) for away, ref in zip(aways, b_refs) for low in range(X_LO)]
    add_products(place_ref, owner_ref, own_ref, partner_ref, sides, None, out_ref, *scratch)


def far_products(away, place_ref, owner_ref, own_ref, partner_ref, near_ref, *refs):
    b_refs, (out_ref, total, *scratch) = refs[:X_LO], refs[X_LO:]
    sides = [(away, low, ref) for low, ref in enumerate(b_refs)]
    add_products(place_ref, owner_ref, own_ref, partner_ref, sides, near_ref, total, *scratch)
    out_ref[...] = total[...].astype(out_ref.dtype)


def block_products(place, owner, a_own, a_partner, b_pieces):
    slots, edge = owner.shape[0], a_own.shape[-1]
    smem = pl.BlockSpec(memory_space=pltpu.SMEM)
    vmem = pl.BlockSpec(memory_space=pltpu.VMEM)
    far = len(b_pieces) // 2
    aways = [t for t in range(len(b_pieces)) if t != far]
    shape = (slots, 2, edge, edge)

    def scratch(sides):
        return [
            pltpu.VMEM((8 * sides, edge), jnp.int32),
            pltpu.SMEM((8 * sides, edge), jnp.int32),
            pltpu.SemaphoreType.DMA,
        ]

    def cost(sides):
        products = 2 * sides * (b_pieces[0].shape[1] // edge // 2)
        return pl.CostEstimate(flops=8 * products * edge**3, bytes_accessed=2**20, transcendentals=0)

    common = (place, owner, a_own, a_partner)
    near = pl.pallas_call(
        functools.partial(near_products, aways),
        out_shape=jax.ShapeDtypeStruct(shape, jnp.float32),
        in_specs=[smem, smem, vmem, vmem] + [vmem] * len(aways),
        out_specs=vmem,
        scratch_shapes=scratch(X_LO * len(aways)),
        compiler_params=pltpu.CompilerParams(vmem_limit_bytes=6 * 1024 * 1024),
        cost_estimate=cost(X_LO * len(aways)),
    )(*common, *[b_pieces[t] for t in aways])
    return pl.pallas_call(
        functools.partial(far_products, far),
        out_shape=jax.ShapeDtypeStruct(shape, jnp.bfloat16),
        in_specs=[smem, smem, vmem, vmem, vmem] + [vmem] * X_LO,
        out_specs=vmem,
        scratch_shapes=[pltpu.VMEM(shape, jnp.float32)] + scratch(X_LO),
        compiler_params=pltpu.CompilerParams(vmem_limit_bytes=6 * 1024 * 1024),
        cost_estimate=cost(X_LO),
    )(*common, near, *b_pieces[far])


def around(piece, axis):
    n = lax.axis_size(axis)
    up = [(i, (i + 1) % n) for i in range(n)]
    down = [(i, (i - 1) % n) for i in range(n)]
    found = [piece] + [None] * (n - 1)
    for t in range(1, (n - 1) // 2 + 1):
        found[t] = lax.ppermute(found[t - 1], axis, up)
        found[n - t] = lax.ppermute(found[(n - t + 1) % n], axis, down)
    far = n // 2
    found[far] = (
        lax.ppermute(found[far - 1][0], axis, up),
        lax.ppermute(found[(far + 1) % n][1], axis, down),
    )
    return found


def shards(a_blocks, a_rows, b_blocks, b_cols, owner):
    edge = a_blocks.shape[-1]
    panels = lax.axis_size(ROW)
    group = b_blocks.shape[2]
    a_own = jnp.where(a_rows[0, 0] < BR, a_blocks[0, 0], jnp.zeros_like(a_blocks[0, 0]))
    labels = jnp.pad(b_cols.reshape(1, -1).astype(jnp.bfloat16), ((0, 15), (0, edge - 2 * group)))
    b_own = jnp.concatenate([b_blocks.reshape(-1, edge), labels])

    b_other = lax.ppermute(b_own, "x_lo", [(0, 1), (1, 0)])
    low = lax.axis_index("x_lo")
    b_pair = jnp.where(low == 0, jnp.stack([b_own, b_other]), jnp.stack([b_other, b_own]))
    plane = ("x_hi", "y")
    a_half = lax.all_to_all(
        jnp.broadcast_to(a_own[None], (lax.axis_size(plane),) + a_own.shape), plane, split_axis=0, concat_axis=0, tiled=True
    )
    partner = lax.ppermute(a_half, "core", [(0, 1), (1, 0)])

    b_pieces = around(b_pair, "z")
    base = (group * lax.axis_index(COL) + lax.axis_index(ROW)) % panels
    place = jnp.stack([base, lax.axis_index("z"), lax.axis_index("core")]).astype(jnp.int32)
    outgoing = block_products(place, owner[0, 0], a_half, partner, b_pieces)
    arrived = lax.all_to_all(outgoing, COL[::-1], split_axis=0, concat_axis=0, tiled=True)
    arrived = arrived.reshape(X_LO, -1, 2, edge, edge).transpose(2, 1, 0, 3, 4)
    return arrived.reshape(2, 1, 1, -1, edge, edge)


def solution(mesh):
    rows, columns = mesh.devices.shape
    fine = Mesh(
        mesh.devices.reshape(rows // (X_HI * CORES), X_HI, CORES, columns // X_LO, X_LO), ROW + COL
    )
    in_specs = (
        P(COL, ROW, None, None),
        P(COL, ROW),
        P(None, ROW, COL, None, None),
        P(None, ROW, COL),
        P(COL, ROW, None),
    )
    out_specs = P(None, COL, ROW, None, None, None)
    return jax.shard_map(shards, mesh=fine, in_specs=in_specs, out_specs=out_specs, check_vma=False)
```
